32 devices in a mesh: seq: 8 (over z, y), res: 4 (over x, core).
Axes of the slice: x: 2, y: 2, z: 4, core: 2. Of those that a mesh axis runs over, the one named last changes fastest.
Arguments:
- homolog_profile: bfloat16 [64, 512, 256], P('seq', 'res'), may hold values from -6 to 6
- couplings_tensor: bfloat16 [512, 512, 128], P('res', 'seq'), may hold values from -6 to 6
- present_entries: int32 [64, 512], P('seq', 'res'), may hold values 0 or 1
- resolved_positions: int32 [512], P('res'), may hold values 0 or 1
- coupling_logit_matrix: bfloat16 [128, 8], replicated
- horizontal_asking_matrix: bfloat16 [256, 256], replicated
- horizontal_lookup_matrix: bfloat16 [256, 256], replicated, may hold values from -0.375 to 0.375
- horizontal_content_matrix: bfloat16 [256, 256], replicated, may hold values from -0.375 to 0.375
- horizontal_sigmoid_matrix: bfloat16 [256, 256], replicated, may hold values from -0.375 to 0.375
- horizontal_final_matrix: bfloat16 [256, 256], replicated, may hold values from -0.375 to 0.375
- vertical_asking_matrix: bfloat16 [256, 256], replicated
- vertical_lookup_matrix: bfloat16 [256, 256], replicated, may hold values from -0.375 to 0.375
- vertical_content_matrix: bfloat16 [256, 256], replicated, may hold values from -0.375 to 0.375
- vertical_sigmoid_matrix: bfloat16 [256, 256], replicated, may hold values from -0.375 to 0.375
- vertical_final_matrix: bfloat16 [256, 256], replicated, may hold values from -0.375 to 0.375
- widening_matrix: bfloat16 [256, 1024], replicated, may hold values from -0.375 to 0.375
- narrowing_matrix: bfloat16 [1024, 256], replicated, may hold values from -0.1875 to 0.1875
Outputs:
- msa_next: bfloat16 [64, 512, 256], P('seq', 'res')
The draws below stay inside these ranges and needn't reach their ends.
All inputs are finite; a program needn't handle non-finite values. No bound on the sum of `present_entries` or of `resolved_positions` on one device may be relied on, other than what follows from the above.
Results may differ from the reference program's by a relative error of at most 0.014.
The reference program's roundings to bfloat16 on the way count: a program that leaves them out, or rounds other values in their place, can miss the bound.
Values may be sent and summed in bfloat16 or wider, within the bound.
A program may use at most 128 MiB of HBM per device.

```python
import jax
import jax.numpy as jnp
from jax import lax

HEADS = 8
HEAD_DIM = 32
CZ = 128
WIDEN_FACTOR = 4
EMBED_DEPTH = 256
HOMOLOG_NUMBER = 64
CHAIN_POSITIONS = 512
N_RES = 4


def draw_coupling_logit_matrix(key, part):
    key = jax.random.fold_in(key, 11)
    starting_offset = jax.random.truncated_normal(key, -4.0, 4.0, (CZ, HEADS), jnp.float32) * (3.0 * CZ ** (-0.5))
    return starting_offset.astype(jnp.bfloat16)


def draw_horizontal_asking_matrix(key, part):
    key = jax.random.fold_in(key, 12)
    starting_offset = jax.random.truncated_normal(key, -4.0, 4.0, (EMBED_DEPTH, EMBED_DEPTH), jnp.float32) * EMBED_DEPTH ** (-0.5)
    return starting_offset.astype(jnp.bfloat16)


def draw_vertical_asking_matrix(key, part):
    key = jax.random.fold_in(key, 13)
    starting_offset = jax.random.truncated_normal(key, -4.0, 4.0, (EMBED_DEPTH, EMBED_DEPTH), jnp.float32) * EMBED_DEPTH ** (-0.5)
    return starting_offset.astype(jnp.bfloat16)


def plant(entries, stream_key, low, high):
    shape = entries.shape
    spot = [jax.random.randint(jax.random.fold_in(stream_key, axis), (), 0, shape[axis]) for axis in range(len(shape))]
    entries = entries.at[tuple(spot)].set(low)
    longest = shape.index(max(shape))
    spot[longest] = (spot[longest] + 1) % shape[longest]
    return entries.at[tuple(spot)].set(high)


def level_of(own_key, shape, pieces, smallest, largest):
    def one(position, blocks):
        draws = jax.random.uniform(jax.random.fold_in(jax.random.fold_in(own_key, 6), position), (blocks,), jnp.float32, smallest / len(pieces), largest / len(pieces))
        return jnp.repeat(jnp.exp(draws), shape[position] // blocks).reshape((-1,) + (1,) * (len(shape) - position - 1))

    loudness = one(*pieces[0])
    for cut in pieces[1:]:
        loudness = loudness * one(*cut)
    return loudness


def scatter_about(key, extent, scale, most, shards=(), kind=jnp.bfloat16):
    gain = level_of(key, extent, shards, -0.22, 0.18) if shards else 1.0
    array = jax.random.normal(key, extent, jnp.float32) * scale * gain
    return jnp.minimum(jnp.maximum(array, -most), most).astype(kind)


def setup_inputs(seed: int = 0) -> dict:
    splits = jax.random.split(jax.random.key(seed), 18)
    return {
        "homolog_profile": scatter_about(splits[0], (HOMOLOG_NUMBER, CHAIN_POSITIONS, EMBED_DEPTH), 1.0, 6.0, ((0, 8), (1, 4))),
        "couplings_tensor": scatter_about(splits[1], (CHAIN_POSITIONS, CHAIN_POSITIONS, CZ), 1.0, 6.0, ((0, 4), (1, 8))),
        "present_entries": plant((jax.random.randint(splits[2], (HOMOLOG_NUMBER, CHAIN_POSITIONS), 0, 8) < 7).astype(jnp.int32), jax.random.fold_in(splits[2], 1), 0, 1),
        "resolved_positions": plant((jax.random.randint(splits[3], (CHAIN_POSITIONS,), 0, 16) < 15).astype(jnp.int32), jax.random.fold_in(splits[3], 1), 0, 1),
        "coupling_logit_matrix": draw_coupling_logit_matrix(jax.random.fold_in(splits[17], 71), 0),
        "horizontal_asking_matrix": draw_horizontal_asking_matrix(jax.random.fold_in(splits[17], 71), 0),
        "horizontal_lookup_matrix": scatter_about(splits[6], (EMBED_DEPTH, EMBED_DEPTH), EMBED_DEPTH ** -0.5, 0.375),
        "horizontal_content_matrix": scatter_about(splits[7], (EMBED_DEPTH, EMBED_DEPTH), EMBED_DEPTH ** -0.5, 0.375),
        "horizontal_sigmoid_matrix": scatter_about(splits[8], (EMBED_DEPTH, EMBED_DEPTH), EMBED_DEPTH ** -0.5, 0.375),
        "horizontal_final_matrix": scatter_about(splits[9], (EMBED_DEPTH, EMBED_DEPTH), EMBED_DEPTH ** -0.5, 0.375),
        "vertical_asking_matrix": draw_vertical_asking_matrix(jax.random.fold_in(splits[17], 71), 0),
        "vertical_lookup_matrix": scatter_about(splits[11], (EMBED_DEPTH, EMBED_DEPTH), EMBED_DEPTH ** -0.5, 0.375),
        "vertical_content_matrix": scatter_about(splits[12], (EMBED_DEPTH, EMBED_DEPTH), EMBED_DEPTH ** -0.5, 0.375),
        "vertical_sigmoid_matrix": scatter_about(splits[13], (EMBED_DEPTH, EMBED_DEPTH), EMBED_DEPTH ** -0.5, 0.375),
        "vertical_final_matrix": scatter_about(splits[14], (EMBED_DEPTH, EMBED_DEPTH), EMBED_DEPTH ** -0.5, 0.375),
        "widening_matrix": scatter_about(splits[15], (EMBED_DEPTH, WIDEN_FACTOR * EMBED_DEPTH), EMBED_DEPTH ** -0.5, 0.375),
        "narrowing_matrix": scatter_about(splits[16], (WIDEN_FACTOR * EMBED_DEPTH, EMBED_DEPTH), (WIDEN_FACTOR * EMBED_DEPTH) ** -0.5, 0.1875),
    }


EPS = 1e-05
MASK_SCALE = 1000000000.0

def standardize_features_fn(values):
    values = values.astype(jnp.float32)
    center = values - lax.optimization_barrier(jnp.mean(values, -1, keepdims=True))
    spread = lax.optimization_barrier(jnp.mean(center * center, -1, keepdims=True))
    return center * lax.rsqrt(spread + EPS)

def bias_rows(block, coupling_logit_matrix):
    return jnp.einsum('ijc,ch->hij', standardize_features_fn(block), coupling_logit_matrix.astype(jnp.float32), precision=lax.Precision.HIGHEST).astype(jnp.bfloat16)

def rounded_weights(probs):
    low = lax.optimization_barrier(probs.astype(jnp.bfloat16))
    return low.astype(jnp.float32)

def column_block(inputs, okay, w_query, w_key, w_value, w_gate):
    number_entries, homolog_groups, embedding_depth = inputs.shape
    head_dim = embedding_depth // HEADS
    scale = HEAD_DIM ** (-0.5)
    query = (jnp.dot(inputs, w_query, preferred_element_type=jnp.float32) * scale).astype(jnp.bfloat16)
    keys = jnp.dot(inputs, w_key, preferred_element_type=jnp.float32).astype(jnp.bfloat16)
    values = jnp.dot(inputs, w_value, preferred_element_type=jnp.float32).astype(jnp.bfloat16)
    gate = jax.nn.sigmoid(jnp.dot(inputs, w_gate, preferred_element_type=jnp.float32))
    query = query.reshape(number_entries, homolog_groups, HEADS, head_dim).astype(jnp.float32)
    keys = keys.reshape(number_entries, homolog_groups, HEADS, head_dim).astype(jnp.float32)
    values = values.reshape(number_entries, homolog_groups, HEADS, head_dim).astype(jnp.float32)
    masking = ((okay.astype(jnp.float32) - 1.0) * MASK_SCALE).T
    score = jnp.einsum('sihd,tihd->ihst', query, keys) + masking[:, None, None, :]
    probs = jnp.exp(score - lax.optimization_barrier(jnp.max(score, -1, keepdims=True)))
    total = lax.optimization_barrier(jnp.sum(probs, -1))
    mixed = jnp.einsum('ihst,tihd->sihd', rounded_weights(probs), values)
    mixed = mixed / jnp.transpose(total, (2, 0, 1))[..., None]
    return (mixed.reshape(number_entries, homolog_groups, embedding_depth) * gate).astype(jnp.bfloat16)

def reference(homolog_profile, couplings_tensor, present_entries, resolved_positions, coupling_logit_matrix, horizontal_asking_matrix, horizontal_lookup_matrix, horizontal_content_matrix, horizontal_sigmoid_matrix, horizontal_final_matrix, vertical_asking_matrix, vertical_lookup_matrix, vertical_content_matrix, vertical_sigmoid_matrix, vertical_final_matrix, widening_matrix, narrowing_matrix):
    number_entries, stretch_extent, embedding_depth = homolog_profile.shape
    head_dim = embedding_depth // HEADS
    scale = HEAD_DIM ** (-0.5)
    blocks = couplings_tensor.reshape(N_RES, stretch_extent // N_RES, stretch_extent, CZ)
    bias = lax.map(lambda block: bias_rows(block, coupling_logit_matrix), blocks)
    bias = jnp.transpose(bias, (1, 0, 2, 3)).reshape(HEADS, stretch_extent, stretch_extent)
    lone_source_tensor = standardize_features_fn(homolog_profile).astype(jnp.bfloat16)
    query = (jnp.dot(lone_source_tensor, horizontal_asking_matrix, preferred_element_type=jnp.float32) * scale).astype(jnp.bfloat16)
    keys = jnp.dot(lone_source_tensor, horizontal_lookup_matrix, preferred_element_type=jnp.float32).astype(jnp.bfloat16)
    values = jnp.dot(lone_source_tensor, horizontal_content_matrix, preferred_element_type=jnp.float32).astype(jnp.bfloat16)
    gate = jax.nn.sigmoid(jnp.dot(lone_source_tensor, horizontal_sigmoid_matrix, preferred_element_type=jnp.float32))
    key_valid = present_entries * resolved_positions[None, :]

    def row_one(items):
        qq, kk, vv, ok = items
        qq = qq.reshape(stretch_extent, HEADS, head_dim).astype(jnp.float32)
        kk = kk.reshape(stretch_extent, HEADS, head_dim).astype(jnp.float32)
        vv = vv.reshape(stretch_extent, HEADS, head_dim).astype(jnp.float32)
        score = jnp.einsum('ihd,jhd->hij', qq, kk) + bias.astype(jnp.float32)
        score = score + ((ok.astype(jnp.float32) - 1.0) * MASK_SCALE)[None, None, :]
        probs = jnp.exp(score - lax.optimization_barrier(jnp.max(score, -1, keepdims=True)))
        total = lax.optimization_barrier(jnp.sum(probs, -1))
        mixed = jnp.einsum('hij,jhd->ihd', rounded_weights(probs), vv)
        mixed = mixed / jnp.transpose(total)[..., None]
        return mixed.reshape(stretch_extent, embedding_depth)
    row_mixed = lax.map(row_one, (query, keys, values, key_valid))
    lone_head_mixing = (row_mixed * gate).astype(jnp.bfloat16)
    lone_homolog_group = homolog_profile.astype(jnp.float32) + jnp.dot(lone_head_mixing, horizontal_final_matrix, preferred_element_type=jnp.float32)
    second_activations = standardize_features_fn(lone_homolog_group).astype(jnp.bfloat16)
    split_parts = stretch_extent // N_RES
    x_blocks = jnp.moveaxis(second_activations.reshape(number_entries, N_RES, split_parts, embedding_depth), 1, 0)
    valid_blocks = jnp.moveaxis(present_entries.reshape(number_entries, N_RES, split_parts), 1, 0)
    second_mixing = lax.map(lambda items: column_block(items[0], items[1], vertical_asking_matrix, vertical_lookup_matrix, vertical_content_matrix, vertical_sigmoid_matrix), (x_blocks, valid_blocks))
    second_mixing = jnp.moveaxis(second_mixing, 0, 1).reshape(number_entries, stretch_extent, embedding_depth)
    updated_profile = lone_homolog_group + jnp.dot(second_mixing, vertical_final_matrix, preferred_element_type=jnp.float32)
    x_three = standardize_features_fn(updated_profile).astype(jnp.bfloat16)
    hidden = jax.nn.relu(jnp.dot(x_three, widening_matrix, preferred_element_type=jnp.float32)).astype(jnp.bfloat16)
    return (updated_profile + jnp.dot(hidden, narrowing_matrix, preferred_element_type=jnp.float32)).astype(jnp.bfloat16)
```

```python
import functools

import jax
import jax.numpy as jnp
from jax import lax
from jax.experimental import pallas as pl
from jax.experimental.pallas import tpu as pltpu
from jax.sharding import PartitionSpec as P

HEADS = 8
HEAD_DIM = 32
EPS = 1e-05
MASK_SCALE = 1000000000.0
MESH = pl.DeviceIdType.MESH
BF16 = jnp.bfloat16
F32 = jnp.float32


def norm(v):
    center = v - jnp.mean(v, -1, keepdims=True)
    spread = jnp.mean(center * center, -1, keepdims=True)
    return center * lax.rsqrt(spread + EPS)


def mm(a, b):
    return jnp.dot(a, b, preferred_element_type=F32)


def mm_t(a, b):
    return lax.dot_general(a, b, (((1,), (1,)), ((), ())), preferred_element_type=F32)


def head_mask(rows, channels, h):
    lane = lax.broadcasted_iota(jnp.int32, (rows, channels), 1)
    return (lane >= h * HEAD_DIM) & (lane < (h + 1) * HEAD_DIM)


class Gather:
    def __init__(self, axis, n, buf, send, recv):
        self.axis, self.n, self.buf, self.send, self.recv = axis, n, buf, send, recv
        self.me = lax.axis_index(axis)
        self.sib = self.me + 1 - 2 * lax.rem(self.me, 2)
        self.far = n // 2 - 1

    def copy(self, slot, sem, to):
        return pltpu.make_async_remote_copy(
            src_ref=self.buf.at[slot],
            dst_ref=self.buf.at[slot],
            send_sem=self.send.at[sem],
            recv_sem=self.recv.at[slot],
            device_id={self.axis: to},
            device_id_type=MESH,
        )

    def source(self, t):
        return lax.rem(self.me + self.n - 2 * t, self.n)

    def start(self):
        for t in range(1, self.far + 1):
            self.copy(self.me, t, lax.rem(self.me + 2 * t, self.n)).start()
        self.copy(self.me, 0, self.sib).start()

    def forward(self, t):
        src = self.source(t)
        c = self.copy(src, self.far + t, self.sib)
        c.wait_recv()
        c.start()

    def finish(self, t):
        src = lax.rem(self.sib + self.n - 2 * t, self.n)
        self.copy(src, 0, self.sib).wait_recv()
        return src

    def drain(self):
        for t in range(2 * self.far + 1):
            self.copy(self.me, t, self.sib).wait_send()


def kernel(
    n_seq,
    n_res,
    hp,
    cp,
    present,
    resolved,
    wz,
    wq,
    wk,
    wv,
    wg,
    wo,
    cq,
    ck,
    cv,
    cg,
    co,
    wide,
    narrow,
    out,
    prof,
    rmask,
    cmask,
    cmask_t,
    bstage,
    brecv,
    ball,
    q1,
    g1,
    k1,
    v1,
    m1b,
    x2s,
    x2t,
    xf,
    q2,
    k2,
    v2,
    g2,
    af,
    a2s,
    a2r,
    prof_send,
    prof_recv,
    rm_send,
    rm_recv,
    cm_send,
    cm_recv,
    b_send,
    b_recv,
    f_send,
    f_recv,
    r_send,
    r_recv,
):
    entries, groups, depth = hp.shape
    parts, rows, jb, _ = cp.shape
    ni = groups // n_seq
    many = n_seq * entries
    scale = HEAD_DIM ** (-0.5)
    me = lax.axis_index("seq")
    mine = lax.axis_index("res")

    barrier = pltpu.get_barrier_semaphore()
    for t in range(1, n_seq):
        pl.semaphore_signal(
            barrier, inc=1, device_id={"seq": lax.rem(me + t, n_seq)}, device_id_type=MESH
        )
    for t in range(1, n_res):
        pl.semaphore_signal(
            barrier, inc=1, device_id={"res": lax.rem(mine + t, n_res)}, device_id_type=MESH
        )

    prof[mine] = hp[...]
    here = present[...]
    rmask[mine] = ((here * resolved[...]).astype(F32) - 1.0) * MASK_SCALE
    cmask[me] = (here.astype(F32) - 1.0) * MASK_SCALE
    pl.semaphore_wait(barrier, n_seq - 1 + n_res - 1)

    gp = Gather("res", n_res, prof, prof_send, prof_recv)
    gr = Gather("res", n_res, rmask, rm_send, rm_recv)
    gc = Gather("seq", n_seq, cmask, cm_send, cm_recv)
    gb = Gather("seq", n_seq, brecv, b_send, b_recv)
    gr.start()
    gc.start()
    gp.start()

    step = 8

    def bias_block(b, carry):
        wide_rows = cp[:, pl.ds(b * step, step)].astype(F32)
        x = norm(wide_rows.reshape(parts * step * jb, wide_rows.shape[-1]))
        x = x.reshape(parts, step, jb, x.shape[-1])
        high = x.astype(BF16)
        low = (x - high.astype(F32)).astype(BF16)
        for k in range(step):
            hi = jnp.concatenate([high[a, k] for a in range(parts)], 0)
            lo = jnp.concatenate([low[a, k] for a in range(parts)], 0)
            piece = mm_t(wz[...], hi) + mm_t(wz[...], lo)
            bstage[pl.ds(b * step + k, HEADS, stride=rows), :] = piece[:HEADS]
        return carry

    lax.fori_loop(0, rows // step, bias_block, 0)
    brecv[me] = bstage[...].astype(BF16)
    gb.start()

    def own_side(s, carry):
        x = norm(hp[s].astype(F32)).astype(BF16)
        q1[s] = (mm(x, wq[...]) * scale).astype(BF16)
        g1[s] = jax.nn.sigmoid(mm(x, wg[...]))
        return carry

    lax.fori_loop(0, entries, own_side, 0)

    def key_side(r):
        start = pl.multiple_of(r * groups, groups)

        def one(s, carry):
            x = norm(prof[r, s].astype(F32)).astype(BF16)
            k1[s, pl.ds(start, groups), :] = mm(x, wk[...]).astype(BF16)
            v1[s, pl.ds(start, groups), :] = mm(x, wv[...]).astype(BF16)
            return carry

        lax.fori_loop(0, entries, one, 0)

    key_side(mine)
    if gb.far >= 1:
        gb.forward(1)
    for t in range(1, gp.far + 1):
        gr.forward(t)
        gp.forward(t)
    for t in range(2, gb.far + 1):
        gb.forward(t)
    for t in range(1, gc.far + 1):
        gc.forward(t)
    for t in range(1, gp.far + 1):
        key_side(gp.source(t))
    for t in range(0, gp.far + 1):
        key_side(gp.finish(t))
        gr.finish(t)
    for t in range(0, gc.far + 1):
        gc.finish(t)
    for t in range(0, gb.far + 1):
        gb.finish(t)

    cmask_t[...] = jnp.transpose(cmask[...].reshape(many, groups))

    if parts == 2:
        first = lax.broadcasted_iota(jnp.int32, (rows, 2 * jb), 1) < jb
        for h in range(HEADS):
            for c in range(n_seq // 2):
                left = brecv[2 * c, h * rows : (h + 1) * rows, :].astype(F32)
                right = brecv[2 * c + 1, h * rows : (h + 1) * rows, :].astype(F32)
                top = jnp.where(first, left, pltpu.roll(right, jb, 1))
                low = jnp.where(first, pltpu.roll(left, jb, 1), right)
                cols = slice(c * 2 * jb, (c + 1) * 2 * jb)
                ball[h, :rows, cols] = top.astype(BF16)
                ball[h, rows:, cols] = low.astype(BF16)

    def bias_of(h):
        if parts == 2:
            return ball[h].astype(F32)
        return jnp.concatenate(
            [brecv[c, h * rows : (h + 1) * rows, :] for c in range(n_seq)], 1
        ).astype(F32)

    hmask = [head_mask(groups, depth, h) for h in range(HEADS)]

    def row(s, carry):
        q = q1[s]
        kk = k1[s]
        vv = v1[s]
        masking = jnp.concatenate([rmask[r, pl.ds(s, 1), :] for r in range(n_res)], 1)
        acc = jnp.zeros((groups, depth), F32)
        for h in range(HEADS):
            qh = jnp.where(hmask[h], q, jnp.zeros_like(q))
            score = mm_t(qh, kk) + bias_of(h) + masking
            probs = jnp.exp(score - jnp.max(score, -1, keepdims=True))
            total = jnp.sum(probs, -1, keepdims=True)
            mixed = mm(probs.astype(BF16), vv)
            acc = jnp.where(hmask[h], mixed / total, acc)
        a1 = (acc * g1[s]).astype(BF16)
        m1 = hp[s].astype(F32) + mm(a1, wo[...])
        x2 = norm(m1)
        for p in range(n_seq):
            m1b[p, s] = m1[p * ni : (p + 1) * ni]
            x2s[p, s] = x2[p * ni : (p + 1) * ni].astype(BF16)
        for t in range(1, n_seq):
            to = lax.rem(me + t, n_seq)
            pltpu.make_async_remote_copy(
                src_ref=x2s.at[to, s],
                dst_ref=x2t.at[me, s],
                send_sem=f_send.at[t],
                recv_sem=f_recv.at[me],
                device_id={"seq": to},
                device_id_type=MESH,
            ).start()
        return carry

    lax.fori_loop(0, entries, row, 0)

    def whole_copy(t, src, dst, send, recv):
        origin = lax.rem(me + n_seq - t, n_seq)
        to = lax.rem(me + t, n_seq)
        return pltpu.make_async_remote_copy(
            src_ref=src.at[to],
            dst_ref=dst.at[origin],
            send_sem=send.at[t],
            recv_sem=recv.at[origin],
            device_id={"seq": to},
            device_id_type=MESH,
        )

    x2t[me] = x2s[me]
    for t in range(1, n_seq):
        whole_copy(t, x2s, x2t, f_send, f_recv).wait_recv()

    half = 128
    halves = depth // half
    for c in range(n_seq):
        x = x2t[c].astype(F32).reshape(entries * ni, depth)
        for e in range(halves):
            xf[e, c * entries * ni : (c + 1) * entries * ni, :] = x[:, e * half : (e + 1) * half]

    for i in range(ni):
        x = jnp.concatenate(
            [xf[e, pl.ds(i, many, stride=ni), :] for e in range(halves)], 1
        ).astype(BF16)
        q2[i] = (mm(x, cq[...]) * scale).astype(BF16)
        k2[i] = mm(x, ck[...]).astype(BF16)
        v2[i] = mm(x, cv[...]).astype(BF16)
        g2[i] = jax.nn.sigmoid(mm(x, cg[...]))

    cm = [head_mask(many, depth, h) for h in range(HEADS)]

    def column(i, carry):
        q = q2[i]
        masking = cmask_t[pl.ds(me * ni + i, 1), :]
        stacked = jnp.concatenate([jnp.where(m, q, jnp.zeros_like(q)) for m in cm], 0)
        score = mm_t(stacked, k2[i]) + masking
        probs = jnp.exp(score - jnp.max(score, -1, keepdims=True))
        total = jnp.sum(probs, -1, keepdims=True)
        mixed = mm(probs.astype(BF16), v2[i]) / total
        acc = mixed[:many]
        for h in range(1, HEADS):
            acc = jnp.where(cm[h], mixed[h * many : (h + 1) * many], acc)
        acc = acc * g2[i]
        for e in range(halves):
            af[e, pl.ds(pl.multiple_of(i * many, many), many), :] = acc[:, e * half : (e + 1) * half]
        return carry

    lax.fori_loop(0, ni, column, 0)

    for s in range(many):
        x = jnp.concatenate(
            [af[e, pl.ds(s, ni, stride=many), :] for e in range(halves)], 1
        )
        a2s[s // entries, s % entries] = x.astype(BF16)

    for t in range(1, n_seq):
        to = lax.rem(me + t, n_seq)
        pltpu.make_async_remote_copy(
            src_ref=a2s.at[to],
            dst_ref=a2r.at[me],
            send_sem=r_send.at[t],
            recv_sem=r_recv.at[me],
            device_id={"seq": to},
            device_id_type=MESH,
        ).start()
    a2r[me] = a2s[me]
    for t in range(1, n_seq):
        whole_copy(t, a2s, a2r, r_send, r_recv).wait_recv()

    pair = 2
    for c in range(0, n_seq, pair):
        a2 = a2r[c : c + pair].astype(F32).reshape(pair * entries * ni, depth).astype(BF16)
        m2 = m1b[c : c + pair].reshape(pair * entries * ni, depth) + mm(a2, co[...])
        x3 = norm(m2).astype(BF16)
        hid = jnp.maximum(mm(x3, wide[...]), 0.0).astype(BF16)
        res = (m2 + mm(hid, narrow[...])).reshape(pair, entries, ni, depth)
        for e in range(pair):
            out[:, (c + e) * ni : (c + e + 1) * ni, :] = res[e].astype(BF16)

    for g in (gp, gr, gc, gb):
        g.drain()
    for t in range(1, n_seq):
        whole_copy(t, x2s, x2t, f_send, f_recv).wait_send()
        whole_copy(t, a2s, a2r, r_send, r_recv).wait_send()


def on_device(n_seq, n_res, hp, cp, present, resolved, wz, *weights):
    entries, groups, depth = hp.shape
    jb = cp.shape[1]
    parts = 128 // jb
    rows = groups // parts
    total = n_res * groups
    ni = groups // n_seq
    many = n_seq * entries
    vm = pltpu.VMEM
    dma = pltpu.SemaphoreType.DMA
    scratch = [
        vm((n_res, entries, groups, depth), BF16),
        vm((n_res, entries, groups), F32),
        vm((n_seq, entries, groups), F32),
        vm((groups, many), F32),
        vm((HEADS * rows, 128), F32),
        vm((n_seq, HEADS * rows, 128), BF16),
        vm((HEADS, groups, total) if parts == 2 else (1, 16, 128), BF16),
        vm((entries, groups, depth), BF16),
        vm((entries, groups, depth), F32),
        vm((entries, total, depth), BF16),
        vm((entries, total, depth), BF16),
        vm((n_seq, entries, ni, depth), F32),
        vm((n_seq, entries, ni, depth), BF16),
        vm((n_seq, entries, ni, depth), BF16),
        vm((depth // 128, many * ni, 128), F32),
        vm((ni, many, depth), BF16),
        vm((ni, many, depth), BF16),
        vm((ni, many, depth), BF16),
        vm((ni, many, depth), F32),
        vm((depth // 128, many * ni, 128), F32),
        vm((n_seq, entries, ni, depth), BF16),
        vm((n_seq, entries, ni, depth), BF16),
    ]
    for n in (n_res, n_res, n_seq, n_seq, n_seq, n_seq):
        scratch += [dma((n,)), dma((n,))]
    operands = (
        hp,
        cp.reshape(parts, rows, jb, cp.shape[-1]),
        present,
        resolved.reshape(1, groups),
        jnp.pad(wz.T, ((0, 8), (0, 0))),
        *weights,
    )
    spec = pl.BlockSpec(memory_space=pltpu.VMEM)
    return pl.pallas_call(
        functools.partial(kernel, n_seq, n_res),
        out_shape=jax.ShapeDtypeStruct(hp.shape, BF16),
        in_specs=[spec] * len(operands),
        out_specs=spec,
        scratch_shapes=scratch,
        compiler_params=pltpu.CompilerParams(
            collective_id=0, has_side_effects=True, vmem_limit_bytes=60 * 1024 * 1024
        ),
    )(*operands)


def solution(mesh):
    placed = (P("seq", "res", None), P("res", "seq", None), P("seq", "res"), P("res"))
    return jax.shard_map(
        functools.partial(on_device, mesh.shape["seq"], mesh.shape["res"]),
        mesh=mesh,
        in_specs=placed + (P(),) * 13,
        out_specs=P("seq", "res", None),
        check_vma=False,
    )
```

```python
import functools

import jax
import jax.numpy as jnp
from jax import lax
from jax.experimental import pallas as pl
from jax.experimental.pallas import tpu as pltpu
from jax.sharding import PartitionSpec as P

HEADS = 8
HEAD_DIM = 32
EPS = 1e-05
MASK_SCALE = 1000000000.0
CHUNKS = 2
TOGETHER = 4
MESH = pl.DeviceIdType.MESH
BF16 = jnp.bfloat16
F32 = jnp.float32


def norm(v):
    center = v - jnp.mean(v, -1, keepdims=True)
    spread = jnp.mean(center * center, -1, keepdims=True)
    return center * lax.rsqrt(spread + EPS)


def mm(a, b):
    return jnp.dot(a, b, preferred_element_type=F32)


def mm_t(a, b):
    return lax.dot_general(a, b, (((1,), (1,)), ((), ())), preferred_element_type=F32)


def head_mask(rows, channels, h):
    lane = lax.broadcasted_iota(jnp.int32, (rows, channels), 1)
    return (lane >= h * HEAD_DIM) & (lane < (h + 1) * HEAD_DIM)


class Gather:
    def __init__(self, axis, n, buf, send, recv):
        self.axis, self.n, self.buf, self.send, self.recv = axis, n, buf, send, recv
        self.me = lax.axis_index(axis)
        self.sib = self.me + 1 - 2 * lax.rem(self.me, 2)
        self.far = n // 2 - 1

    def copy(self, slot, sem, to):
        return pltpu.make_async_remote_copy(
            src_ref=self.buf.at[slot],
            dst_ref=self.buf.at[slot],
            send_sem=self.send.at[sem],
            recv_sem=self.recv.at[slot],
            device_id={self.axis: to},
            device_id_type=MESH,
        )

    def source(self, t):
        return lax.rem(self.me + self.n - 2 * t, self.n)

    def start(self):
        for t in range(1, self.far + 1):
            self.copy(self.me, t, lax.rem(self.me + 2 * t, self.n)).start()
        self.copy(self.me, 0, self.sib).start()

    def forward(self, t):
        src = self.source(t)
        c = self.copy(src, self.far + t, self.sib)
        c.wait_recv()
        c.start()

    def finish(self, t):
        src = lax.rem(self.sib + self.n - 2 * t, self.n)
        self.copy(src, 0, self.sib).wait_recv()
        return src

    def drain(self):
        for t in range(2 * self.far + 1):
            self.copy(self.me, t, self.sib).wait_send()


def kernel(
    n_seq,
    n_res,
    hp,
    cp,
    present,
    resolved,
    wz,
    wq,
    wk,
    wv,
    wg,
    wo,
    cq,
    ck,
    cv,
    cg,
    co,
    wide,
    narrow,
    out,
    prof,
    rmask,
    cmask,
    cmask_t,
    bstage,
    brecv,
    ball,
    q1,
    g1,
    k1,
    v1,
    m1b,
    x2s,
    x2t,
    xf,
    q2,
    k2,
    v2,
    g2,
    a2s,
    a2r,
    prof_send,
    prof_recv,
    rm_send,
    rm_recv,
    cm_send,
    cm_recv,
    b_send,
    b_recv,
    f_send,
    f_recv,
    r_send,
    r_recv,
):
    entries, groups, depth = hp.shape
    parts, rows, jb, _ = cp.shape
    ni = groups // n_seq
    many = n_seq * entries
    scale = HEAD_DIM ** (-0.5)
    half = 128
    halves = depth // half
    me = lax.axis_index("seq")
    mine = lax.axis_index("res")

    barrier = pltpu.get_barrier_semaphore()
    for t in range(1, n_seq):
        pl.semaphore_signal(
            barrier, inc=1, device_id={"seq": lax.rem(me + t, n_seq)}, device_id_type=MESH
        )
    for t in range(1, n_res):
        pl.semaphore_signal(
            barrier, inc=1, device_id={"res": lax.rem(mine + t, n_res)}, device_id_type=MESH
        )

    prof[mine] = hp[...]
    here = present[...]
    rmask[mine] = ((here * resolved[...]).astype(F32) - 1.0) * MASK_SCALE
    cmask[me] = (here.astype(F32) - 1.0) * MASK_SCALE
    pl.semaphore_wait(barrier, n_seq - 1 + n_res - 1)

    gp = Gather("res", n_res, prof, prof_send, prof_recv)
    gr = Gather("res", n_res, rmask, rm_send, rm_recv)
    gc = Gather("seq", n_seq, cmask, cm_send, cm_recv)
    gbs = [
        Gather("seq", n_seq, brecv.at[a], b_send.at[a], b_recv.at[a]) for a in range(CHUNKS)
    ]
    gr.start()
    gc.start()
    gp.start()

    step = 8
    some = rows // CHUNKS
    wzt = jnp.transpose(wz[...].astype(F32)).astype(BF16)

    def bias_block(a, b, carry):
        wide_rows = cp[:, pl.ds(a * some + b * step, step)].astype(F32)
        x = norm(wide_rows.reshape(parts * step * jb, wide_rows.shape[-1]))
        x = x.reshape(parts, step, jb, x.shape[-1])
        high = x.astype(BF16)
        low = (x - high.astype(F32)).astype(BF16)
        for k in range(step):
            hi = jnp.concatenate([high[e, k] for e in range(parts)], 0)
            lo = jnp.concatenate([low[e, k] for e in range(parts)], 0)
            piece = mm_t(wzt, hi) + mm_t(wzt, lo)
            bstage[pl.ds(b * step + k, HEADS, stride=some), :] = piece
        return carry

    for a in range(CHUNKS):
        lax.fori_loop(0, some // step, functools.partial(bias_block, a), 0)
        brecv[a, me] = bstage[...].astype(BF16)
        gbs[a].start()

    def own_side(s, carry):
        x = norm(hp[s].astype(F32)).astype(BF16)
        q1[s] = (mm(x, wq[...]) * scale).astype(BF16)
        g1[s] = jax.nn.sigmoid(mm(x, wg[...]))
        return carry

    lax.fori_loop(0, entries, own_side, 0)

    def key_side(r):
        start = pl.multiple_of(r * groups, groups)

        def one(s, carry):
            x = norm(prof[r, s].astype(F32)).astype(BF16)
            k1[s, pl.ds(start, groups), :] = mm(x, wk[...]).astype(BF16)
            v1[s, pl.ds(start, groups), :] = mm(x, wv[...]).astype(BF16)
            return carry

        lax.fori_loop(0, entries, one, 0)

    key_side(mine)
    for t in range(1, gbs[0].far + 1):
        gbs[0].forward(t)
    for t in range(1, gp.far + 1):
        gr.forward(t)
        gp.forward(t)
    for t in range(1, gbs[1].far + 1):
        gbs[1].forward(t)
    for t in range(1, gc.far + 1):
        gc.forward(t)
    for t in range(1, gp.far + 1):
        key_side(gp.source(t))
    for t in range(0, gp.far + 1):
        key_side(gp.finish(t))
        gr.finish(t)
    for t in range(0, gc.far + 1):
        gc.finish(t)
    for gb in gbs:
        for t in range(0, gb.far + 1):
            gb.finish(t)

    cmask_t[...] = jnp.transpose(cmask[...].reshape(many, groups))

    if parts == 2:
        first = lax.broadcasted_iota(jnp.int32, (some, 2 * jb), 1) < jb
        for h in range(HEADS):
            for c in range(n_seq // 2):
                cols = slice(c * 2 * jb, (c + 1) * 2 * jb)
                for a in range(CHUNKS):
                    left = brecv[a, 2 * c, h * some : (h + 1) * some, :].astype(F32)
                    right = brecv[a, 2 * c + 1, h * some : (h + 1) * some, :].astype(F32)
                    top = jnp.where(first, left, pltpu.roll(right, jb, 1))
                    low = jnp.where(first, pltpu.roll(left, jb, 1), right)
                    ball[h, a * some : (a + 1) * some, cols] = top.astype(BF16)
                    ball[h, rows + a * some : rows + (a + 1) * some, cols] = low.astype(BF16)

    def bias_of(h):
        if parts == 2:
            return ball[h].astype(F32)
        return jnp.concatenate(
            [
                jnp.concatenate(
                    [brecv[a, c, h * some : (h + 1) * some, :] for c in range(n_seq)], 1
                )
                for a in range(CHUNKS)
            ],
            0,
        ).astype(F32)

    hmask = [head_mask(groups, depth, h) for h in range(HEADS)]

    def row(s, carry):
        q = q1[s]
        kk = k1[s]
        vv = v1[s]
        masking = jnp.concatenate([rmask[r, pl.ds(s, 1), :] for r in range(n_res)], 1)
        acc = jnp.zeros((groups, depth), F32)
        for first_head in range(0, HEADS, TOGETHER):
            heads = range(first_head, first_head + TOGETHER)
            stacked = jnp.concatenate(
                [jnp.where(hmask[h], q, jnp.zeros_like(q)) for h in heads], 0
            )
            scores = mm_t(stacked, kk)
            weights, inverses = [], []
            for e, h in enumerate(heads):
                score = scores[e * groups : (e + 1) * groups] + bias_of(h) + masking
                probs = jnp.exp(score - jnp.max(score, -1, keepdims=True))
                inverses.append(1.0 / jnp.sum(probs, -1, keepdims=True))
                weights.append(probs.astype(BF16))
            mixed = mm(jnp.concatenate(weights, 0), vv)
            for e, h in enumerate(heads):
                acc = jnp.where(
                    hmask[h], mixed[e * groups : (e + 1) * groups] * inverses[e], acc
                )
        a1 = (acc * g1[s]).astype(BF16)
        m1 = hp[s].astype(F32) + mm(a1, wo[...])
        x2 = norm(m1)
        for e in range(halves):
            m1b[e, pl.ds(s, groups, stride=entries), :] = m1[:, e * half : (e + 1) * half]
        for p in range(n_seq):
            x2s[p, s] = x2[p * ni : (p + 1) * ni].astype(BF16)
        for t in range(1, n_seq):
            to = lax.rem(me + t, n_seq)
            pltpu.make_async_remote_copy(
                src_ref=x2s.at[to, s],
                dst_ref=x2t.at[me, s],
                send_sem=f_send.at[t],
                recv_sem=f_recv.at[me],
                device_id={"seq": to},
                device_id_type=MESH,
            ).start()
        return carry

    lax.fori_loop(0, entries, row, 0)

    def whole_copy(t, src, dst, send, recv):
        origin = lax.rem(me + n_seq - t, n_seq)
        to = lax.rem(me + t, n_seq)
        return pltpu.make_async_remote_copy(
            src_ref=src.at[to],
            dst_ref=dst.at[origin],
            send_sem=send.at[t],
            recv_sem=recv.at[origin],
            device_id={"seq": to},
            device_id_type=MESH,
        )

    x2t[me] = x2s[me]
    for t in range(1, n_seq):
        whole_copy(t, x2s, x2t, f_send, f_recv).wait_recv()

    for c in range(n_seq):
        x = x2t[c].astype(F32).reshape(entries * ni, depth)
        for e in range(halves):
            xf[e, c * entries * ni : (c + 1) * entries * ni, :] = x[:, e * half : (e + 1) * half]

    x = jnp.concatenate(
        [
            jnp.concatenate([xf[e, pl.ds(i, many, stride=ni), :] for e in range(halves)], 1)
            for i in range(ni)
        ],
        0,
    ).astype(BF16)
    q2[...] = (mm(x, cq[...]) * scale).astype(BF16).reshape(q2.shape)
    k2[...] = mm(x, ck[...]).astype(BF16).reshape(k2.shape)
    v2[...] = mm(x, cv[...]).astype(BF16).reshape(v2.shape)
    g2[...] = jax.nn.sigmoid(mm(x, cg[...])).reshape(g2.shape)

    cm = [head_mask(many, depth, h) for h in range(HEADS)]

    def column(i):
        q = q2[i]
        masking = cmask_t[pl.ds(me * ni + i, 1), :]
        stacked = jnp.concatenate([jnp.where(m, q, jnp.zeros_like(q)) for m in cm], 0)
        score = mm_t(stacked, k2[i]) + masking
        probs = jnp.exp(score - jnp.max(score, -1, keepdims=True))
        inverse = 1.0 / jnp.sum(probs, -1, keepdims=True)
        mixed = mm(probs.astype(BF16), v2[i]) * inverse
        acc = mixed[:many]
        for h in range(1, HEADS):
            acc = jnp.where(cm[h], mixed[h * many : (h + 1) * many], acc)
        return acc * g2[i]

    def column_pair(u, carry):
        one, two = column(2 * u), column(2 * u + 1)
        for p in range(n_seq):
            rng = slice(p * entries, (p + 1) * entries)
            a2s[p, u] = jnp.concatenate([one[rng], two[rng]], 0).astype(BF16)
        for t in range(1, n_seq):
            to = lax.rem(me + t, n_seq)
            pltpu.make_async_remote_copy(
                src_ref=a2s.at[to, u],
                dst_ref=a2r.at[me, u],
                send_sem=r_send.at[t],
                recv_sem=r_recv.at[me],
                device_id={"seq": to},
                device_id_type=MESH,
            ).start()
        return carry

    lax.fori_loop(0, ni // 2, column_pair, 0)

    a2r[me] = a2s[me]
    for t in range(1, n_seq):
        whole_copy(t, a2s, a2r, r_send, r_recv).wait_recv()

    pair = 2
    size = pair * ni * entries
    for c in range(0, n_seq, pair):
        rng = slice(c * ni * entries, c * ni * entries + size)
        a2 = a2r[c : c + pair].reshape(size, depth)
        m1 = jnp.concatenate([m1b[e, rng, :] for e in range(halves)], 1)
        m2 = m1 + mm(a2, co[...])
        x3 = norm(m2).astype(BF16)
        hid = jnp.maximum(mm(x3, wide[...]), 0.0).astype(BF16)
        res = m2 + mm(hid, narrow[...])
        for e in range(halves):
            m1b[e, rng, :] = res[:, e * half : (e + 1) * half]
        for s in range(entries):
            for e in range(halves):
                out[s, c * ni : (c + pair) * ni, e * half : (e + 1) * half] = m1b[
                    e, pl.ds(c * ni * entries + s, pair * ni, stride=entries), :
                ].astype(BF16)

    for g in [gp, gr, gc] + gbs:
        g.drain()
    for t in range(1, n_seq):
        whole_copy(t, x2s, x2t, f_send, f_recv).wait_send()
        whole_copy(t, a2s, a2r, r_send, r_recv).wait_send()


def on_device(n_seq, n_res, hp, cp, present, resolved, wz, *weights):
    entries, groups, depth = hp.shape
    jb = cp.shape[1]
    parts = 128 // jb
    rows = groups // parts
    total = n_res * groups
    ni = groups // n_seq
    many = n_seq * entries
    vm = pltpu.VMEM
    dma = pltpu.SemaphoreType.DMA
    scratch = [
        vm((n_res, entries, groups, depth), BF16),
        vm((n_res, entries, groups), F32),
        vm((n_seq, entries, groups), F32),
        vm((groups, many), F32),
        vm((HEADS * rows // CHUNKS, 128), F32),
        vm((CHUNKS, n_seq, HEADS * rows // CHUNKS, 128), BF16),
        vm((HEADS, groups, total) if parts == 2 else (1, 16, 128), BF16),
        vm((entries, groups, depth), BF16),
        vm((entries, groups, depth), F32),
        vm((entries, total, depth), BF16),
        vm((entries, total, depth), BF16),
        vm((depth // 128, groups * entries, 128), F32),
        vm((n_seq, entries, ni, depth), BF16),
        vm((n_seq, entries, ni, depth), BF16),
        vm((depth // 128, many * ni, 128), F32),
        vm((ni, many, depth), BF16),
        vm((ni, many, depth), BF16),
        vm((ni, many, depth), BF16),
        vm((ni, many, depth), F32),
        vm((n_seq, ni // 2, 2 * entries, depth), BF16),
        vm((n_seq, ni // 2, 2 * entries, depth), BF16),
    ]
    for n in ((n_res,), (n_res,), (n_seq,), (CHUNKS, n_seq), (n_seq,), (n_seq,)):
        scratch += [dma(n), dma(n)]
    operands = (
        hp,
        cp.reshape(parts, rows, jb, cp.shape[-1]),
        present,
        resolved.reshape(1, groups),
        wz,
        *weights,
    )
    spec = pl.BlockSpec(memory_space=pltpu.VMEM)
    return pl.pallas_call(
        functools.partial(kernel, n_seq, n_res),
        out_shape=jax.ShapeDtypeStruct(hp.shape, BF16),
        in_specs=[spec] * len(operands),
        out_specs=spec,
        scratch_shapes=scratch,
        compiler_params=pltpu.CompilerParams(
            collective_id=0, has_side_effects=True, vmem_limit_bytes=60 * 1024 * 1024
        ),
    )(*operands)


def solution(mesh):
    placed = (P("seq", "res", None), P("res", "seq", None), P("seq", "res"), P("res"))
    return jax.shard_map(
        functools.partial(on_device, mesh.shape["seq"], mesh.shape["res"]),
        mesh=mesh,
        in_specs=placed + (P(),) * 13,
        out_specs=P("seq", "res", None),
        check_vma=False,
    )
```

```python
import functools

import jax
import jax.numpy as jnp
from jax import lax
from jax.experimental import pallas as pl
from jax.experimental.pallas import tpu as pltpu
from jax.sharding import PartitionSpec as P

HEADS = 8
HEAD_DIM = 32
EPS = 1e-05
MASK_SCALE = 1000000000.0
CHUNKS = 4
TOGETHER = 4
SEQS = 4
COLS = 4
MESH = pl.DeviceIdType.MESH
BF16 = jnp.bfloat16
F32 = jnp.float32


def norm(v):
    center = v - jnp.mean(v, -1, keepdims=True)
    spread = jnp.mean(center * center, -1, keepdims=True)
    return center * lax.rsqrt(spread + EPS)


def mm(a, b):
    return jnp.dot(a, b, preferred_element_type=F32)


def mm_t(a, b):
    return lax.dot_general(a, b, (((1,), (1,)), ((), ())), preferred_element_type=F32)


def head_mask(rows, channels, h):
    lane = lax.broadcasted_iota(jnp.int32, (rows, channels), 1)
    return (lane >= h * HEAD_DIM) & (lane < (h + 1) * HEAD_DIM)


class Gather:
    def __init__(self, axis, n, buf, send, recv):
        self.axis, self.n, self.buf, self.send, self.recv = axis, n, buf, send, recv
        self.me = lax.axis_index(axis)
        self.sib = self.me + 1 - 2 * lax.rem(self.me, 2)
        self.far = n // 2 - 1

    def copy(self, slot, sem, to):
        return pltpu.make_async_remote_copy(
            src_ref=self.buf.at[slot],
            dst_ref=self.buf.at[slot],
            send_sem=self.send.at[sem],
            recv_sem=self.recv.at[slot],
            device_id={self.axis: to},
            device_id_type=MESH,
        )

    def source(self, t):
        return lax.rem(self.me + self.n - 2 * t, self.n)

    def start(self):
        for t in range(1, self.far + 1):
            self.copy(self.me, t, lax.rem(self.me + 2 * t, self.n)).start()
        self.copy(self.me, 0, self.sib).start()

    def forward(self, t):
        src = self.source(t)
        c = self.copy(src, self.far + t, self.sib)
        c.wait_recv()
        c.start()

    def finish(self, t):
        src = lax.rem(self.sib + self.n - 2 * t, self.n)
        self.copy(src, 0, self.sib).wait_recv()
        return src

    def drain(self):
        for t in range(2 * self.far + 1):
            self.copy(self.me, t, self.sib).wait_send()


def kernel(
    n_seq,
    n_res,
    hp,
    cp,
    present,
    resolved,
    wz,
    wq,
    wk,
    wv,
    wg,
    wo,
    cq,
    ck,
    cv,
    cg,
    co,
    wide,
    narrow,
    out,
    prof,
    rmask,
    cmask,
    cmask_t,
    bstage,
    brecv,
    ball,
    q1,
    g1,
    k1,
    v1,
    m1b,
    x2s,
    x2t,
    xf,
    q2,
    k2,
    v2,
    g2,
    a2s,
    a2r,
    prof_send,
    prof_recv,
    rm_send,
    rm_recv,
    cm_send,
    cm_recv,
    b_send,
    b_recv,
    f_send,
    f_recv,
    r_send,
    r_recv,
):
    entries, groups, depth = hp.shape
    parts, rows, jb, _ = cp.shape
    ni = groups // n_seq
    many = n_seq * entries
    scale = HEAD_DIM ** (-0.5)
    half = 128
    halves = depth // half
    me = lax.axis_index("seq")
    mine = lax.axis_index("res")

    barrier = pltpu.get_barrier_semaphore()
    for t in range(1, n_seq):
        pl.semaphore_signal(
            barrier, inc=1, device_id={"seq": lax.rem(me + t, n_seq)}, device_id_type=MESH
        )
    for t in range(1, n_res):
        pl.semaphore_signal(
            barrier, inc=1, device_id={"res": lax.rem(mine + t, n_res)}, device_id_type=MESH
        )

    prof[mine] = hp[...]
    here = present[...]
    rmask[mine] = ((here * resolved[...]).astype(F32) - 1.0) * MASK_SCALE
    cmask[me] = (here.astype(F32) - 1.0) * MASK_SCALE
    pl.semaphore_wait(barrier, n_seq - 1 + n_res - 1)

    gp = Gather("res", n_res, prof, prof_send, prof_recv)
    gr = Gather("res", n_res, rmask, rm_send, rm_recv)
    gc = Gather("seq", n_seq, cmask, cm_send, cm_recv)
    gbs = [
        Gather("seq", n_seq, brecv.at[a], b_send.at[a], b_recv.at[a]) for a in range(CHUNKS)
    ]
    gr.start()
    gc.start()
    gp.start()

    step = 8
    some = rows // CHUNKS
    wzt = wz[...]

    def bias_block(a, b, carry):
        wide_rows = cp[:, pl.ds(a * some + b * step, step)].astype(F32)
        x = norm(wide_rows.reshape(parts * step * jb, wide_rows.shape[-1]))
        x = x.reshape(parts, step, jb, x.shape[-1])
        high = x.astype(BF16)
        low = (x - high.astype(F32)).astype(BF16)
        for k in range(step):
            hi = jnp.concatenate([high[e, k] for e in range(parts)], 0)
            lo = jnp.concatenate([low[e, k] for e in range(parts)], 0)
            piece = mm_t(wzt, hi) + mm_t(wzt, lo)
            bstage[pl.ds(b * step + k, HEADS, stride=some), :] = piece
        return carry

    for a in range(CHUNKS):
        lax.fori_loop(0, some // step, functools.partial(bias_block, a), 0)
        brecv[a, me] = bstage[...].astype(BF16)
        gbs[a].start()

    def own_side(u, carry):
        rng = pl.ds(u * SEQS, SEQS)
        x = norm(hp[rng].astype(F32).reshape(SEQS * groups, depth)).astype(BF16)
        q1[rng] = (mm(x, wq[...]) * scale).astype(BF16).reshape(SEQS, groups, depth)
        g1[rng] = jax.nn.sigmoid(mm(x, wg[...])).reshape(SEQS, groups, depth)
        return carry

    lax.fori_loop(0, entries // SEQS, own_side, 0)

    def key_side(r):
        keys = pl.ds(pl.multiple_of(r * groups, groups), groups)

        def some_seqs(u, carry):
            rng = pl.ds(u * SEQS, SEQS)
            x = norm(prof[r, rng].astype(F32).reshape(SEQS * groups, depth)).astype(BF16)
            k1[rng, keys, :] = mm(x, wk[...]).astype(BF16).reshape(SEQS, groups, depth)
            v1[rng, keys, :] = mm(x, wv[...]).astype(BF16).reshape(SEQS, groups, depth)
            return carry

        lax.fori_loop(0, entries // SEQS, some_seqs, 0)

    key_side(mine)
    for gb in gbs[: CHUNKS // 2]:
        for t in range(1, gb.far + 1):
            gb.forward(t)
    for t in range(1, gp.far + 1):
        gr.forward(t)
        gp.forward(t)
    for gb in gbs[CHUNKS // 2 :]:
        for t in range(1, gb.far + 1):
            gb.forward(t)
    for t in range(1, gc.far + 1):
        gc.forward(t)
    for t in range(1, gp.far + 1):
        key_side(gp.source(t))
    for t in range(0, gp.far + 1):
        key_side(gp.finish(t))
        gr.finish(t)
    for t in range(0, gc.far + 1):
        gc.finish(t)

    cmask_t[...] = jnp.transpose(cmask[...].reshape(many, groups))

    first = lax.broadcasted_iota(jnp.int32, (some, 2 * jb), 1) < jb
    for a, gb in enumerate(gbs):
        for t in range(0, gb.far + 1):
            gb.finish(t)
        if parts == 2:
            for h in range(HEADS):
                for c in range(n_seq // 2):
                    cols = slice(c * 2 * jb, (c + 1) * 2 * jb)
                    left = brecv[a, 2 * c, h * some : (h + 1) * some, :].astype(F32)
                    right = brecv[a, 2 * c + 1, h * some : (h + 1) * some, :].astype(F32)
                    top = jnp.where(first, left, pltpu.roll(right, jb, 1))
                    low = jnp.where(first, pltpu.roll(left, jb, 1), right)
                    ball[h, a * some : (a + 1) * some, cols] = top.astype(BF16)
                    ball[h, rows + a * some : rows + (a + 1) * some, cols] = low.astype(BF16)

    def bias_of(h):
        if parts == 2:
            return ball[h].astype(F32)
        return jnp.concatenate(
            [
                jnp.concatenate(
                    [brecv[a, c, h * some : (h + 1) * some, :] for c in range(n_seq)], 1
                )
                for a in range(CHUNKS)
            ],
            0,
        ).astype(F32)

    hmask = [head_mask(groups, depth, h) for h in range(HEADS)]

    def row(s):
        q = q1[s]
        kk = k1[s]
        vv = v1[s]
        masking = jnp.concatenate([rmask[r, pl.ds(s, 1), :] for r in range(n_res)], 1)
        acc = jnp.zeros((groups, depth), F32)
        for first_head in range(0, HEADS, TOGETHER):
            heads = range(first_head, first_head + TOGETHER)
            stacked = jnp.concatenate(
                [jnp.where(hmask[h], q, jnp.zeros_like(q)) for h in heads], 0
            )
            scores = mm_t(stacked, kk)
            weights, inverses = [], []
            for e, h in enumerate(heads):
                score = scores[e * groups : (e + 1) * groups] + bias_of(h) + masking
                probs = jnp.exp(score - jnp.max(score, -1, keepdims=True))
                inverses.append(1.0 / jnp.sum(probs, -1, keepdims=True))
                weights.append(probs.astype(BF16))
            mixed = mm(jnp.concatenate(weights, 0), vv)
            for e, h in enumerate(heads):
                acc = jnp.where(
                    hmask[h], mixed[e * groups : (e + 1) * groups] * inverses[e], acc
                )
        a1 = (acc * g1[s]).astype(BF16)
        m1 = hp[s].astype(F32) + mm(a1, wo[...])
        return m1, norm(m1)

    def row_pair(u, carry):
        results = [row(2 * u), row(2 * u + 1)]
        for z, (m1, x2) in enumerate(results):
            s = 2 * u + z
            for e in range(halves):
                m1b[e, pl.ds(s, groups, stride=entries), :] = m1[:, e * half : (e + 1) * half]
            for p in range(n_seq):
                x2s[p, s] = x2[p * ni : (p + 1) * ni].astype(BF16)
        for t in range(1, n_seq):
            to = lax.rem(me + t, n_seq)
            pltpu.make_async_remote_copy(
                src_ref=x2s.at[to, pl.ds(2 * u, 2)],
                dst_ref=x2t.at[me, pl.ds(2 * u, 2)],
                send_sem=f_send.at[t],
                recv_sem=f_recv.at[me],
                device_id={"seq": to},
                device_id_type=MESH,
            ).start()
        return carry

    lax.fori_loop(0, entries // 2, row_pair, 0)

    def whole_copy(t, src, dst, send, recv):
        origin = lax.rem(me + n_seq - t, n_seq)
        to = lax.rem(me + t, n_seq)
        return pltpu.make_async_remote_copy(
            src_ref=src.at[to],
            dst_ref=dst.at[origin],
            send_sem=send.at[t],
            recv_sem=recv.at[origin],
            device_id={"seq": to},
            device_id_type=MESH,
        )

    x2t[me] = x2s[me]
    for t in range(1, n_seq):
        whole_copy(t, x2s, x2t, f_send, f_recv).wait_recv()

    for c in range(n_seq):
        x = x2t[c].astype(F32).reshape(entries * ni, depth)
        for e in range(halves):
            xf[e, c * entries * ni : (c + 1) * entries * ni, :] = x[:, e * half : (e + 1) * half]

    x = jnp.concatenate(
        [
            jnp.concatenate([xf[e, pl.ds(i, many, stride=ni), :] for e in range(halves)], 1)
            for i in range(ni)
        ],
        0,
    ).astype(BF16)
    q2[...] = (mm(x, cq[...]) * scale).astype(BF16).reshape(q2.shape)
    k2[...] = mm(x, ck[...]).astype(BF16).reshape(k2.shape)
    v2[...] = mm(x, cv[...]).astype(BF16).reshape(v2.shape)
    g2[...] = jax.nn.sigmoid(mm(x, cg[...])).reshape(g2.shape)

    cm = [head_mask(many, depth, h) for h in range(HEADS)]

    def column(i):
        q = q2[i]
        masking = cmask_t[pl.ds(me * ni + i, 1), :]
        stacked = jnp.concatenate([jnp.where(m, q, jnp.zeros_like(q)) for m in cm], 0)
        score = mm_t(stacked, k2[i]) + masking
        probs = jnp.exp(score - jnp.max(score, -1, keepdims=True))
        inverse = 1.0 / jnp.sum(probs, -1, keepdims=True)
        mixed = mm(probs.astype(BF16), v2[i]) * inverse
        acc = mixed[:many]
        for h in range(1, HEADS):
            acc = jnp.where(cm[h], mixed[h * many : (h + 1) * many], acc)
        return acc * g2[i]

    pairs = COLS // 2

    def column_group(u, carry):
        done = [column(COLS * u + z) for z in range(COLS)]
        for p in range(n_seq):
            rng = slice(p * entries, (p + 1) * entries)
            for z in range(pairs):
                a2s[p, pairs * u + z] = jnp.concatenate(
                    [done[2 * z][rng], done[2 * z + 1][rng]], 0
                ).astype(BF16)
        for t in range(1, n_seq):
            to = lax.rem(me + t, n_seq)
            pltpu.make_async_remote_copy(
                src_ref=a2s.at[to, pl.ds(pairs * u, pairs)],
                dst_ref=a2r.at[me, pl.ds(pairs * u, pairs)],
                send_sem=r_send.at[t],
                recv_sem=r_recv.at[me],
                device_id={"seq": to},
                device_id_type=MESH,
            ).start()
        return carry

    lax.fori_loop(0, ni // COLS, column_group, 0)

    a2r[me] = a2s[me]
    for t in range(1, n_seq):
        whole_copy(t, a2s, a2r, r_send, r_recv).wait_recv()

    pair = 4
    size = pair * ni * entries
    for c in range(0, n_seq, pair):
        rng = slice(c * ni * entries, c * ni * entries + size)
        a2 = a2r[c : c + pair].reshape(size, depth)
        m1 = jnp.concatenate([m1b[e, rng, :] for e in range(halves)], 1)
        m2 = m1 + mm(a2, co[...])
        x3 = norm(m2).astype(BF16)
        hid = jnp.maximum(mm(x3, wide[...]), 0.0).astype(BF16)
        res = m2 + mm(hid, narrow[...])
        for e in range(halves):
            m1b[e, rng, :] = res[:, e * half : (e + 1) * half]
        for s in range(entries):
            for e in range(halves):
                out[s, c * ni : (c + pair) * ni, e * half : (e + 1) * half] = m1b[
                    e, pl.ds(c * ni * entries + s, pair * ni, stride=entries), :
                ].astype(BF16)

    for g in [gp, gr, gc] + gbs:
        g.drain()
    for t in range(1, n_seq):
        whole_copy(t, x2s, x2t, f_send, f_recv).wait_send()
        whole_copy(t, a2s, a2r, r_send, r_recv).wait_send()


def on_device(n_seq, n_res, hp, cp, present, resolved, wz, *weights):
    entries, groups, depth = hp.shape
    jb = cp.shape[1]
    parts = 128 // jb
    rows = groups // parts
    total = n_res * groups
    ni = groups // n_seq
    many = n_seq * entries
    vm = pltpu.VMEM
    dma = pltpu.SemaphoreType.DMA
    scratch = [
        vm((n_res, entries, groups, depth), BF16),
        vm((n_res, entries, groups), F32),
        vm((n_seq, entries, groups), F32),
        vm((groups, many), F32),
        vm((HEADS * rows // CHUNKS, 128), F32),
        vm((CHUNKS, n_seq, HEADS * rows // CHUNKS, 128), BF16),
        vm((HEADS, groups, total) if parts == 2 else (1, 16, 128), BF16),
        vm((entries, groups, depth), BF16),
        vm((entries, groups, depth), F32),
        vm((entries, total, depth), BF16),
        vm((entries, total, depth), BF16),
        vm((depth // 128, groups * entries, 128), F32),
        vm((n_seq, entries, ni, depth), BF16),
        vm((n_seq, entries, ni, depth), BF16),
        vm((depth // 128, many * ni, 128), F32),
        vm((ni, many, depth), BF16),
        vm((ni, many, depth), BF16),
        vm((ni, many, depth), BF16),
        vm((ni, many, depth), F32),
        vm((n_seq, ni // 2, 2 * entries, depth), BF16),
        vm((n_seq, ni // 2, 2 * entries, depth), BF16),
    ]
    for n in ((n_res,), (n_res,), (n_seq,), (CHUNKS, n_seq), (n_seq,), (n_seq,)):
        scratch += [dma(n), dma(n)]
    operands = (
        hp,
        cp.reshape(parts, rows, jb, cp.shape[-1]),
        present,
        resolved.reshape(1, groups),
        wz.T,
        *weights,
    )
    spec = pl.BlockSpec(memory_space=pltpu.VMEM)
    return pl.pallas_call(
        functools.partial(kernel, n_seq, n_res),
        out_shape=jax.ShapeDtypeStruct(hp.shape, BF16),
        in_specs=[spec] * len(operands),
        out_specs=spec,
        scratch_shapes=scratch,
        compiler_params=pltpu.CompilerParams(
            collective_id=0, has_side_effects=True, vmem_limit_bytes=60 * 1024 * 1024
        ),
    )(*operands)


def solution(mesh):
    placed = (P("seq", "res", None), P("res", "seq", None), P("seq", "res"), P("res"))
    return jax.shard_map(
        functools.partial(on_device, mesh.shape["seq"], mesh.shape["res"]),
        mesh=mesh,
        in_specs=placed + (P(),) * 13,
        out_specs=P("seq", "res", None),
        check_vma=False,
    )
```
